32 devices in a mesh: energy: 16 (over z, x, core), slab: 2 (over y).
Axes of the slice: x: 2, y: 2, z: 4, core: 2. Of those that a mesh axis runs over, the one named last changes fastest.
Arguments:
- green_blocks: bfloat16 [2, 12, 12, 256, 128], P(None, None, None, 'energy', 'slab'), may hold values from -6 to 6
- couplings: bfloat16 [12, 12, 2, 1024], P(None, None, 'slab', 'energy'), may hold values from -1.75 to 1.75
- band_weights: float32 [9, 2, 1024], P(None, 'slab', 'energy'), may hold values from 0.02 to 0.2
- neighbours: int32 [2, 1024], P('slab', 'energy'), may hold values from 0 to 127, as said below
- shifts: int32 [2, 1024], P('slab', 'energy'), may hold values from -32 to 32
Outputs:
- self_energy: bfloat16 [2, 12, 12, 256, 128], P(None, None, None, 'energy', 'slab')
The draws below stay inside these ranges and needn't reach their ends.
Inputs may be any that keep to these rules, and one draw needn't show every extreme that they name: `neighbours`: the partner of each coupling of atom a lies within 4 atoms of a; partners of one atom may repeat.
All inputs are finite; a program needn't handle non-finite values.
Results may differ from the reference program's by a relative error of at most 0.0057.
Values may be sent and summed in bfloat16 or wider, within the bound.
A program may use at most 128 MiB of HBM per device.

```python
import math
import jax
import jax.numpy as jnp
from jax import lax

ORB = 12
ENERGIES = 256
NBR = 16
BAND = 9
SHIFT = 32
HALO = 4
SLABS = 2
ATOMS = 128
PAIRS_SLAB = 1024


def draw_neighbours(key, part):
    pair_index = jnp.arange(SLABS * PAIRS_SLAB, dtype=jnp.int32)
    atom_index = pair_index // NBR
    slot_index = pair_index % NBR
    offset = jax.random.randint(key, (SLABS * PAIRS_SLAB,), -HALO, HALO + 1, dtype=jnp.int32)
    offset = jnp.where(slot_index == 0, 0, jnp.where(slot_index == 1, -HALO, jnp.where(slot_index == 2, HALO, offset)))
    partner = atom_index + offset
    partner = jnp.where(partner < 0, -partner, partner)
    partner = jnp.where(partner > ATOMS - 1, 2 * (ATOMS - 1) - partner, partner)
    return partner.astype(jnp.int32).reshape(SLABS, PAIRS_SLAB)


def with_ends(values, key, low, high):
    longest = values.shape.index(max(values.shape))
    spots = []
    for shift in (0, 1):
        where = [jax.random.randint(jax.random.fold_in(key, axis), (), 0, length) for axis, length in enumerate(values.shape)]
        where[longest] = (where[longest] + shift) % values.shape[longest]
        spots.append(tuple(where))
    return values.at[spots[0]].set(low).at[spots[1]].set(high)


def steps_of(stream_key, extent, shards, low, largest):
    factor_of = 1.0
    for axis_at, shards_of in shards:
        steps = jax.random.uniform(jax.random.fold_in(jax.random.fold_in(stream_key, 6), axis_at), (shards_of,), jnp.float32, low / len(shards), largest / len(shards))
        factor_of = factor_of * jnp.repeat(jnp.exp(steps), extent[axis_at] // shards_of).reshape((-1,) + (1,) * (len(extent) - 1 - axis_at))
    return factor_of


def gaussian(key, dims, scale, bound, shards=(), kind=jnp.bfloat16):
    array = scale * jax.random.normal(key, dims, jnp.float32)
    if shards:
        array = array * steps_of(key, dims, shards, -0.22, 0.18)
    return jnp.clip(array, -bound, bound).astype(kind)


def setup_inputs(seed: int = 0) -> dict:
    keys = jax.random.split(jax.random.key(seed), 6)
    green_blocks = gaussian(keys[0], (2, ORB, ORB, ENERGIES, ATOMS), 1.0, 6.0, ((3, 16), (4, 2)))
    couplings = gaussian(keys[1], (ORB, ORB, SLABS, PAIRS_SLAB), ORB ** -0.5, 1.75, ((2, 2), (3, 16)))
    band_weights = jnp.clip(jnp.exp(math.log(0.2) - 2.3025851 * jax.random.uniform(keys[2], (BAND, SLABS, PAIRS_SLAB), jnp.float32) ** steps_of(keys[2], (BAND, SLABS, PAIRS_SLAB), ((1, 2), (2, 16)), -0.2, 0.2)), 0.02, 0.2)
    neighbours = draw_neighbours(jax.random.fold_in(keys[5], 71), 0)
    shifts = with_ends(jax.random.randint(keys[4], (SLABS, PAIRS_SLAB), 0 - SHIFT, SHIFT + 1), jax.random.fold_in(keys[4], 1), 0 - SHIFT, SHIFT).astype(jnp.int32)
    return dict(green_blocks=green_blocks, couplings=couplings, band_weights=band_weights, neighbours=neighbours, shifts=shifts)


def reference(green_blocks, couplings, band_weights, neighbours, shifts):
    atom_major_in = jnp.transpose(green_blocks, (0, 1, 2, 4, 3))
    atom_count = atom_major_in.shape[3]
    energy_count = atom_major_in.shape[4]
    pad_width = SHIFT + BAND // 2
    padded = jnp.pad(atom_major_in, ((0, 0), (0, 0), (0, 0), (0, 0), (pad_width, pad_width)))
    partner_rows = neighbours.reshape(atom_count, NBR).astype(jnp.int32)
    starts = (shifts.reshape(atom_count, NBR) + pad_width - BAND // 2).astype(jnp.int32)
    band_w = band_weights.reshape(BAND, atom_count, NBR).transpose(1, 2, 0)
    coupling = couplings.reshape(ORB, ORB, atom_count, NBR).transpose(2, 0, 1, 3)
    anchor = jnp.zeros((), jnp.int32)

    def window_of(row, start):
        piece = lax.dynamic_slice(padded, (anchor, anchor, anchor, row, start), (2, ORB, ORB, 1, energy_count + BAND - 1))
        return piece[:, :, :, 0, :]

    def one_atom(per_atom):
        rows_here, starts_here, weight_here, matrix = per_atom
        windows = jax.vmap(window_of, out_axes=3)(rows_here, starts_here)
        summed = jnp.zeros((2, ORB, ORB, NBR, energy_count), jnp.float32)
        for offset in range(BAND):
            summed = summed + weight_here[:, offset][:, None] * windows[..., offset:offset + energy_count].astype(jnp.float32)
        banded = summed.astype(jnp.bfloat16)
        matrix_f = matrix.astype(jnp.float32)
        left_product = jnp.einsum('pqk,cqrkE->cprkE', matrix_f, banded.astype(jnp.float32)).astype(jnp.bfloat16)
        result = jnp.einsum('cprkE,srk->cpsE', left_product.astype(jnp.float32), matrix_f)
        return result.astype(jnp.bfloat16)

    stacked = lax.map(one_atom, (partner_rows, starts, band_w, coupling), batch_size=8)
    return jnp.transpose(stacked, (1, 2, 3, 4, 0))
```

```python
import functools

import jax
import jax.numpy as jnp
from jax import lax
from jax.experimental import pallas as pl
from jax.experimental.pallas import tpu as pltpu
from jax.sharding import PartitionSpec as P

ORB = 12
NBR = 16
BAND = 9
SHIFT = 32
HALO = 4
BLOCK = 2 * ORB * ORB
PAIR = ORB * ORB


def scatter_kernel(near_ref, shift_ref, left_ref, own_ref, right_ref, weight_ref, matrix_ref, out_ref,
                   green, spread_q, spread_r, total):
    per_dev = out_ref.shape[1] // BLOCK
    energies = out_ref.shape[0]
    half = energies // 2
    width = per_dev * BLOCK
    groups = lax.axis_size("energy")
    first_atom = (lax.axis_index("slab") * groups + lax.axis_index("energy")) * per_dev - HALO

    for place, ref in enumerate((left_ref, own_ref, right_ref)):
        green[place * width:(place + 1) * width, :] = ref[...].T

    lane_q = lax.broadcasted_iota(jnp.int32, (128, PAIR), 1)
    row_q = lax.broadcasted_iota(jnp.int32, (128, PAIR), 0)
    pick_q = (lane_q // ORB == row_q).astype(jnp.bfloat16)
    pick_r = (lane_q % ORB == row_q).astype(jnp.bfloat16)
    spread_q[...] = jnp.dot(matrix_ref[...], pick_q, preferred_element_type=jnp.float32).astype(jnp.bfloat16)
    spread_r[...] = jnp.dot(matrix_ref[...], pick_r, preferred_element_type=jnp.float32).astype(jnp.bfloat16)
    row_p = lax.broadcasted_iota(jnp.int32, (PAIR, 16), 0)
    lane_p = lax.broadcasted_iota(jnp.int32, (PAIR, 16), 1)
    pick_p = (row_p // ORB == lane_p).astype(jnp.bfloat16)
    pick_t = (row_p % ORB == lane_p).astype(jnp.bfloat16)
    below = lax.broadcasted_iota(jnp.int32, (half, half), 0) > lax.broadcasted_iota(jnp.int32, (half, half), 1)
    above = lax.broadcasted_iota(jnp.int32, (half, half), 0) < lax.broadcasted_iota(jnp.int32, (half, half), 1)

    sub = lax.broadcasted_iota(jnp.int32, (8, energies), 0)

    def atom(a, carry):
        total[...] = jnp.zeros_like(total)
        for k in range(NBR):
            index = a * NBR + k
            row = weight_ref[pl.ds(index, 1), :]
            turn = lax.rem(2 * energies - BAND // 2 - shift_ref[0, index], energies)
            tile = pltpu.roll(jnp.broadcast_to(row, (8, energies)), turn, 1)
            for step in (1, 2, 4):
                tile = jnp.where((sub & step) != 0, pltpu.roll(tile, step, 1), tile)
            band = jnp.concatenate([pltpu.roll(tile, 8 * b, 1) if b else tile for b in range(half // 8)], axis=0)
            near, far = band[:, :half], band[:, half:]
            near = near.astype(jnp.bfloat16)
            upper = jnp.where(below, far, 0.0).astype(jnp.bfloat16)
            lower = jnp.where(above, far, 0.0).astype(jnp.bfloat16)
            toeplitz = jnp.concatenate([
                jnp.concatenate([near, upper], axis=1),
                jnp.concatenate([lower, near], axis=1)], axis=0)
            partner = near_ref[0, index] - first_atom
            block = green[pl.ds(pl.multiple_of(partner * BLOCK, 32), BLOCK), :]
            banded = jnp.dot(block, toeplitz, preferred_element_type=jnp.float32).astype(jnp.bfloat16)
            rows = pl.ds(pl.multiple_of(index * 16, 16), 16)
            left = jnp.dot(pick_p, spread_q[rows, :], preferred_element_type=jnp.float32)
            right = jnp.dot(pick_t, spread_r[rows, :], preferred_element_type=jnp.float32)
            both = (left * right).astype(jnp.bfloat16)
            for c in range(2):
                part = slice(c * PAIR, (c + 1) * PAIR)
                total[part, :] += jnp.dot(both, banded[part], preferred_element_type=jnp.float32)
        return carry

    for a in range(per_dev):
        atom(a, 0)
        out_ref[:, a * BLOCK:(a + 1) * BLOCK] = total[...].T.astype(jnp.bfloat16)


def on_device(green_blocks, couplings, band_weights, neighbours, shifts):
    groups = lax.axis_size("energy")
    slabs = lax.axis_size("slab")
    local_e, slab_count = green_blocks.shape[3:]
    per_dev = slab_count // groups
    energies = local_e * groups
    width = per_dev * BLOCK
    pairs = per_dev * NBR
    assert per_dev == HALO
    group_pos = lax.axis_index("energy")

    sent = green_blocks.reshape(BLOCK, local_e, groups, per_dev).transpose(2, 1, 3, 0)
    sent = sent.reshape(groups, local_e, width)
    own = lax.all_to_all(sent, "energy", split_axis=0, concat_axis=0, tiled=True).reshape(energies, width)
    chain = [(s, g) for s in range(slabs) for g in range(groups)]
    rank = {pair: pair[1] * slabs + pair[0] for pair in chain}
    up = [(rank[chain[i]], rank[chain[i + 1]]) for i in range(len(chain) - 1)]
    down = [(j, i) for i, j in up]
    left = lax.ppermute(own, ("energy", "slab"), up)
    right = lax.ppermute(own, ("energy", "slab"), down)

    weight = jnp.pad(band_weights.reshape(BAND, pairs)[::-1].T, ((0, 0), (0, energies - BAND)))
    matrix = couplings.reshape(ORB, ORB, pairs).transpose(2, 0, 1)
    matrix = jnp.pad(matrix, ((0, 0), (0, 16 - ORB), (0, 128 - ORB))).reshape(pairs * 16, 128)
    vmem = pl.BlockSpec(memory_space=pltpu.VMEM)
    smem = pl.BlockSpec(memory_space=pltpu.SMEM)
    out = pl.pallas_call(
        scatter_kernel,
        out_shape=jax.ShapeDtypeStruct((energies, width), jnp.bfloat16),
        in_specs=[smem, smem, vmem, vmem, vmem, vmem, vmem],
        out_specs=vmem,
        scratch_shapes=[
            pltpu.VMEM((3 * width, energies), jnp.bfloat16),
            pltpu.VMEM((pairs * 16, PAIR), jnp.bfloat16),
            pltpu.VMEM((pairs * 16, PAIR), jnp.bfloat16),
            pltpu.VMEM((BLOCK, energies), jnp.float32),
        ],
        compiler_params=pltpu.CompilerParams(vmem_limit_bytes=40 * 1024 * 1024),
    )(neighbours, shifts, left, own, right, weight, matrix)
    back = lax.all_to_all(out.reshape(groups, local_e, width), "energy", split_axis=0, concat_axis=0, tiled=True)
    back = back.reshape(groups, local_e, per_dev, BLOCK).transpose(3, 1, 0, 2)
    return back.reshape(2, ORB, ORB, local_e, slab_count)


def solution(mesh):
    return jax.shard_map(
        on_device,
        mesh=mesh,
        in_specs=(
            P(None, None, None, "energy", "slab"),
            P(None, None, "slab", "energy"),
            P(None, "slab", "energy"),
            P("slab", "energy"),
            P("slab", "energy"),
        ),
        out_specs=P(None, None, None, "energy", "slab"),
        check_vma=False,
    )
```

```python
import functools

import jax
import jax.numpy as jnp
from jax import lax
from jax.experimental import pallas as pl
from jax.experimental.pallas import tpu as pltpu
from jax.sharding import PartitionSpec as P

ORB = 12
NBR = 16
BAND = 9
SHIFT = 32
HALO = 4
BLOCK = 2 * ORB * ORB
PAIR = ORB * ORB


MESH = pl.DeviceIdType.MESH


def order(groups, per_dev):
    count = groups * per_dev
    row = lax.broadcasted_iota(jnp.int32, (count, count), 0)
    atom = lax.broadcasted_iota(jnp.int32, (count, count), 1)
    return (atom == (row % groups) * per_dev + row // groups).astype(jnp.bfloat16)


def pack_kernel(groups, per_dev, x_ref, sent, wide, packed):
    local_e = sent.shape[1]
    tiles = wide.shape[0]
    count = x_ref.shape[1]
    lanes = min(count, 128)
    if lanes < 128:
        wide[...] = jnp.zeros_like(wide)
    for j in range(tiles):
        wide[j, :x_ref.shape[0], :lanes] = x_ref[:, j * 128:j * 128 + lanes].astype(jnp.float32)
    pick = order(groups, per_dev)
    for e in range(local_e):
        rows = jnp.concatenate([wide[j, pl.ds(e, BLOCK, stride=local_e), :] for j in range(tiles)], axis=1)
        rows = rows[:, :count].astype(jnp.bfloat16)
        turned = lax.dot_general(pick, rows, (((1,), (1,)), ((), ())), preferred_element_type=jnp.float32)
        flat = jnp.concatenate([turned[i * groups:(i + 1) * groups] for i in range(per_dev)], axis=1)
        for j in range(packed.shape[0]):
            packed[j, pl.ds(e, groups, stride=local_e), :] = flat[:, j * 128:(j + 1) * 128]
    for g in range(groups):
        for j in range(packed.shape[0]):
            sent[g, :, j * 128:(j + 1) * 128] = packed[j, g * local_e:(g + 1) * local_e, :].astype(jnp.bfloat16)


def gather_kernel(groups, x_ref, landed, send_sem, recv_sem):
    me, slab = lax.axis_index("energy"), lax.axis_index("slab")
    barrier = pltpu.get_barrier_semaphore()

    def hello(step, carry):
        pl.semaphore_signal(barrier, inc=1, device_id=(lax.rem(me + step, groups), slab), device_id_type=MESH)
        return carry

    lax.fori_loop(1, groups, hello, 0)
    pl.semaphore_wait(barrier, groups - 1)

    def outgoing(step):
        to = lax.rem(me + step, groups)
        return pltpu.make_async_remote_copy(
            src_ref=x_ref.at[to], dst_ref=landed.at[me], send_sem=send_sem.at[step], recv_sem=recv_sem.at[step],
            device_id=(to, slab), device_id_type=MESH)

    def incoming(step):
        source = lax.rem(me - step + groups, groups)
        return pltpu.make_async_remote_copy(
            src_ref=x_ref.at[source], dst_ref=landed.at[source], send_sem=send_sem.at[step],
            recv_sem=recv_sem.at[step], device_id=(source, slab), device_id_type=MESH)

    def start(step, carry):
        outgoing(step).start()
        return carry

    def finish(step, carry):
        incoming(step).wait_recv()
        outgoing(step).wait_send()
        return carry

    lax.fori_loop(1, groups, start, 0)
    landed[me] = x_ref[me]
    lax.fori_loop(1, groups, finish, 0)


def unpack_kernel(groups, per_dev, landed, out_ref, wide, tall):
    local_e = landed.shape[1]
    lanes = min(out_ref.shape[1], 128)
    for g in range(groups):
        for j in range(wide.shape[0]):
            wide[j, g * local_e:(g + 1) * local_e, :] = landed[g, :, j * 128:(j + 1) * 128].astype(jnp.float32)
    pick = order(groups, per_dev)
    for e in range(local_e):
        rows = jnp.concatenate(
            [wide[j, pl.ds(e, groups, stride=local_e), :] for j in range(wide.shape[0])], axis=1)
        stack = jnp.concatenate([rows[:, i * BLOCK:(i + 1) * BLOCK] for i in range(per_dev)], axis=0)
        turned = jnp.dot(stack.T.astype(jnp.bfloat16), pick, preferred_element_type=jnp.float32)
        if lanes < 128:
            turned = jnp.concatenate([turned, jnp.zeros((BLOCK, 128 - lanes), jnp.float32)], axis=1)
        for j in range(tall.shape[0]):
            tall[j, pl.ds(e, BLOCK, stride=local_e), :] = turned[:, j * 128:(j + 1) * 128]
    for j in range(tall.shape[0]):
        out_ref[:, j * 128:j * 128 + lanes] = tall[j, :out_ref.shape[0], :lanes].astype(jnp.bfloat16)


def scatter_kernel(near_ref, shift_ref, left_ref, own_ref, right_ref, weight_ref, matrix_ref, out_ref,
                   green, spread_q, spread_r, total):
    per_dev = out_ref.shape[1] // BLOCK
    energies = out_ref.shape[0]
    half = energies // 2
    width = per_dev * BLOCK
    groups = lax.axis_size("energy")
    first_atom = (lax.axis_index("slab") * groups + lax.axis_index("energy")) * per_dev - HALO

    for place, ref in enumerate((left_ref, own_ref, right_ref)):
        green[place * width:(place + 1) * width, :] = ref[...].T

    lane_q = lax.broadcasted_iota(jnp.int32, (128, PAIR), 1)
    row_q = lax.broadcasted_iota(jnp.int32, (128, PAIR), 0)
    pick_q = (lane_q // ORB == row_q).astype(jnp.bfloat16)
    pick_r = (lane_q % ORB == row_q).astype(jnp.bfloat16)
    spread_q[...] = jnp.dot(matrix_ref[...], pick_q, preferred_element_type=jnp.float32).astype(jnp.bfloat16)
    spread_r[...] = jnp.dot(matrix_ref[...], pick_r, preferred_element_type=jnp.float32).astype(jnp.bfloat16)
    row_p = lax.broadcasted_iota(jnp.int32, (PAIR, 16), 0)
    lane_p = lax.broadcasted_iota(jnp.int32, (PAIR, 16), 1)
    pick_p = (row_p // ORB == lane_p).astype(jnp.bfloat16)
    pick_t = (row_p % ORB == lane_p).astype(jnp.bfloat16)
    below = lax.broadcasted_iota(jnp.int32, (half, half), 0) > lax.broadcasted_iota(jnp.int32, (half, half), 1)
    above = lax.broadcasted_iota(jnp.int32, (half, half), 0) < lax.broadcasted_iota(jnp.int32, (half, half), 1)

    sub = lax.broadcasted_iota(jnp.int32, (8, energies), 0)

    def atom(a, carry):
        total[...] = jnp.zeros_like(total)
        for k in range(NBR):
            index = a * NBR + k
            row = weight_ref[pl.ds(index, 1), :]
            turn = lax.rem(2 * energies - BAND // 2 - shift_ref[0, index], energies)
            tile = pltpu.roll(jnp.broadcast_to(row, (8, energies)), turn, 1)
            for step in (1, 2, 4):
                tile = jnp.where((sub & step) != 0, pltpu.roll(tile, step, 1), tile)
            band = jnp.concatenate([pltpu.roll(tile, 8 * b, 1) if b else tile for b in range(half // 8)], axis=0)
            near, far = band[:, :half], band[:, half:]
            near = near.astype(jnp.bfloat16)
            upper = jnp.where(below, far, 0.0).astype(jnp.bfloat16)
            lower = jnp.where(above, far, 0.0).astype(jnp.bfloat16)
            toeplitz = jnp.concatenate([
                jnp.concatenate([near, upper], axis=1),
                jnp.concatenate([lower, near], axis=1)], axis=0)
            partner = jnp.clip(near_ref[0, index] - first_atom, 0, 3 * per_dev - 1)
            block = green[pl.ds(pl.multiple_of(partner * BLOCK, 32), BLOCK), :]
            banded = jnp.dot(block, toeplitz, preferred_element_type=jnp.float32).astype(jnp.bfloat16)
            rows = pl.ds(pl.multiple_of(index * 16, 16), 16)
            left = jnp.dot(pick_p, spread_q[rows, :], preferred_element_type=jnp.float32)
            right = jnp.dot(pick_t, spread_r[rows, :], preferred_element_type=jnp.float32)
            both = (left * right).astype(jnp.bfloat16)
            for c in range(2):
                part = slice(c * PAIR, (c + 1) * PAIR)
                total[part, :] += jnp.dot(both, banded[part], preferred_element_type=jnp.float32)
        return carry

    for a in range(per_dev):
        atom(a, 0)
        out_ref[:, a * BLOCK:(a + 1) * BLOCK] = total[...].T.astype(jnp.bfloat16)


def on_device(green_blocks, couplings, band_weights, neighbours, shifts):
    groups = lax.axis_size("energy")
    slabs = lax.axis_size("slab")
    local_e, slab_count = green_blocks.shape[3:]
    per_dev = slab_count // groups
    energies = local_e * groups
    width = per_dev * BLOCK
    pairs = per_dev * NBR
    assert per_dev == HALO
    vmem = pl.BlockSpec(memory_space=pltpu.VMEM)
    smem = pl.BlockSpec(memory_space=pltpu.SMEM)
    blocks = jax.ShapeDtypeStruct((groups, local_e, width), jnp.bfloat16)
    wide = pltpu.VMEM((pl.cdiv(slab_count, 128), BLOCK * local_e, 128), jnp.float32)
    packed = pltpu.VMEM((width // 128, energies, 128), jnp.float32)
    room = pltpu.CompilerParams(vmem_limit_bytes=32 * 1024 * 1024)
    sent = pl.pallas_call(
        functools.partial(pack_kernel, groups, per_dev),
        out_shape=blocks, in_specs=[vmem], out_specs=vmem,
        scratch_shapes=[wide, packed], compiler_params=room,
    )(green_blocks.reshape(BLOCK * local_e, slab_count))
    def exchanged(value, number):
        return pl.pallas_call(
            functools.partial(gather_kernel, groups),
            out_shape=blocks,
            in_specs=[vmem],
            out_specs=vmem,
            scratch_shapes=[
                pltpu.SemaphoreType.DMA((groups,)),
                pltpu.SemaphoreType.DMA((groups,)),
            ],
            compiler_params=pltpu.CompilerParams(
                collective_id=number, has_side_effects=True, vmem_limit_bytes=32 * 1024 * 1024),
        )(value)

    own = exchanged(sent, 0).reshape(energies, width)
    chain = [g * slabs + s for s in range(slabs) for g in range(groups)]
    up = list(zip(chain[:-1], chain[1:]))
    left = lax.ppermute(own, ("energy", "slab"), up)
    right = lax.ppermute(own, ("energy", "slab"), [(j, i) for i, j in up])

    weight = jnp.pad(band_weights.reshape(BAND, pairs)[::-1].T, ((0, 0), (0, energies - BAND)))
    matrix = couplings.reshape(ORB, ORB, pairs).transpose(2, 0, 1)
    matrix = jnp.pad(matrix, ((0, 0), (0, 16 - ORB), (0, 128 - ORB))).reshape(pairs * 16, 128)
    out = pl.pallas_call(
        scatter_kernel,
        out_shape=jax.ShapeDtypeStruct((energies, width), jnp.bfloat16),
        in_specs=[smem, smem, vmem, vmem, vmem, vmem, vmem],
        out_specs=vmem,
        scratch_shapes=[
            pltpu.VMEM((3 * width, energies), jnp.bfloat16),
            pltpu.VMEM((pairs * 16, PAIR), jnp.bfloat16),
            pltpu.VMEM((pairs * 16, PAIR), jnp.bfloat16),
            pltpu.VMEM((BLOCK, energies), jnp.float32),
        ],
        compiler_params=pltpu.CompilerParams(vmem_limit_bytes=40 * 1024 * 1024),
    )(neighbours, shifts, left, own, right, weight, matrix)
    landed = exchanged(out.reshape(groups, local_e, width), 1)
    back = pl.pallas_call(
        functools.partial(unpack_kernel, groups, per_dev),
        out_shape=jax.ShapeDtypeStruct((BLOCK * local_e, slab_count), jnp.bfloat16),
        in_specs=[vmem], out_specs=vmem,
        scratch_shapes=[packed, wide], compiler_params=room,
    )(landed)
    return back.reshape(2, ORB, ORB, local_e, slab_count)


def solution(mesh):
    return jax.shard_map(
        on_device,
        mesh=mesh,
        in_specs=(
            P(None, None, None, "energy", "slab"),
            P(None, None, "slab", "energy"),
            P(None, "slab", "energy"),
            P("slab", "energy"),
            P("slab", "energy"),
        ),
        out_specs=P(None, None, None, "energy", "slab"),
        check_vma=False,
    )
```

```python
import functools

import jax
import jax.numpy as jnp
from jax import lax
from jax.experimental import pallas as pl
from jax.experimental.pallas import tpu as pltpu
from jax.sharding import PartitionSpec as P

ORB = 12
NBR = 16
BAND = 9
SHIFT = 32
HALO = 4
BLOCK = 2 * ORB * ORB
PAIR = ORB * ORB


MESH = pl.DeviceIdType.MESH


def order(groups, per_dev):
    count = groups * per_dev
    row = lax.broadcasted_iota(jnp.int32, (count, count), 0)
    atom = lax.broadcasted_iota(jnp.int32, (count, count), 1)
    return (atom == (row % groups) * per_dev + row // groups).astype(jnp.bfloat16)


def pack_kernel(groups, per_dev, x_ref, sent, wide, packed):
    local_e = sent.shape[1]
    tiles = wide.shape[0]
    count = x_ref.shape[1]
    lanes = min(count, 128)
    if lanes < 128:
        wide[...] = jnp.zeros_like(wide)
    for j in range(tiles):
        wide[j, :x_ref.shape[0], :lanes] = x_ref[:, j * 128:j * 128 + lanes].astype(jnp.float32)
    pick = order(groups, per_dev)
    for e in range(local_e):
        rows = jnp.concatenate([wide[j, pl.ds(e, BLOCK, stride=local_e), :] for j in range(tiles)], axis=1)
        rows = rows[:, :count].astype(jnp.bfloat16)
        turned = lax.dot_general(pick, rows, (((1,), (1,)), ((), ())), preferred_element_type=jnp.float32)
        flat = jnp.concatenate([turned[i * groups:(i + 1) * groups] for i in range(per_dev)], axis=1)
        for j in range(packed.shape[0]):
            packed[j, pl.ds(e, groups, stride=local_e), :] = flat[:, j * 128:(j + 1) * 128]
    for g in range(groups):
        for j in range(packed.shape[0]):
            sent[g, :, j * 128:(j + 1) * 128] = packed[j, g * local_e:(g + 1) * local_e, :].astype(jnp.bfloat16)


def gather_kernel(groups, x_ref, landed, send_sem, recv_sem):
    me, slab = lax.axis_index("energy"), lax.axis_index("slab")
    barrier = pltpu.get_barrier_semaphore()

    def hello(step, carry):
        pl.semaphore_signal(barrier, inc=1, device_id=(lax.rem(me + step, groups), slab), device_id_type=MESH)
        return carry

    lax.fori_loop(1, groups, hello, 0)
    pl.semaphore_wait(barrier, groups - 1)

    def outgoing(step):
        to = lax.rem(me + step, groups)
        return pltpu.make_async_remote_copy(
            src_ref=x_ref.at[to], dst_ref=landed.at[me], send_sem=send_sem.at[step], recv_sem=recv_sem.at[step],
            device_id=(to, slab), device_id_type=MESH)

    def incoming(step):
        source = lax.rem(me - step + groups, groups)
        return pltpu.make_async_remote_copy(
            src_ref=x_ref.at[source], dst_ref=landed.at[source], send_sem=send_sem.at[step],
            recv_sem=recv_sem.at[step], device_id=(source, slab), device_id_type=MESH)

    def start(step, carry):
        outgoing(step).start()
        return carry

    def finish(step, carry):
        incoming(step).wait_recv()
        outgoing(step).wait_send()
        return carry

    lax.fori_loop(1, groups, start, 0)
    landed[me] = x_ref[me]
    lax.fori_loop(1, groups, finish, 0)


def unpack_kernel(groups, per_dev, landed, out_ref, wide, tall):
    local_e = landed.shape[1]
    lanes = min(out_ref.shape[1], 128)
    for g in range(groups):
        for j in range(wide.shape[0]):
            wide[j, g * local_e:(g + 1) * local_e, :] = landed[g, :, j * 128:(j + 1) * 128].astype(jnp.float32)
    pick = order(groups, per_dev)
    for e in range(local_e):
        rows = jnp.concatenate(
            [wide[j, pl.ds(e, groups, stride=local_e), :] for j in range(wide.shape[0])], axis=1)
        stack = jnp.concatenate([rows[:, i * BLOCK:(i + 1) * BLOCK] for i in range(per_dev)], axis=0)
        turned = jnp.dot(stack.T.astype(jnp.bfloat16), pick, preferred_element_type=jnp.float32)
        if lanes < 128:
            turned = jnp.concatenate([turned, jnp.zeros((BLOCK, 128 - lanes), jnp.float32)], axis=1)
        for j in range(tall.shape[0]):
            tall[j, pl.ds(e, BLOCK, stride=local_e), :] = turned[:, j * 128:(j + 1) * 128]
    for j in range(tall.shape[0]):
        out_ref[:, j * 128:j * 128 + lanes] = tall[j, :out_ref.shape[0], :lanes].astype(jnp.bfloat16)


def scatter_kernel(near_ref, shift_ref, left_ref, own_ref, right_ref, weight_ref, matrix_ref, out_ref,
                   green, spread_q, spread_r, total):
    per_dev = out_ref.shape[1] // BLOCK
    energies = out_ref.shape[0]
    half = energies // 2
    width = per_dev * BLOCK
    groups = lax.axis_size("energy")
    first_atom = (lax.axis_index("slab") * groups + lax.axis_index("energy")) * per_dev - HALO

    for place, ref in enumerate((left_ref, own_ref, right_ref)):
        green[place * width:(place + 1) * width, :] = ref[...].T

    lane_q = lax.broadcasted_iota(jnp.int32, (128, PAIR), 1)
    row_q = lax.broadcasted_iota(jnp.int32, (128, PAIR), 0)
    pick_q = (lane_q // ORB == row_q).astype(jnp.bfloat16)
    pick_r = (lane_q % ORB == row_q).astype(jnp.bfloat16)
    spread_q[...] = jnp.dot(matrix_ref[...], pick_q, preferred_element_type=jnp.float32).astype(jnp.bfloat16)
    spread_r[...] = jnp.dot(matrix_ref[...], pick_r, preferred_element_type=jnp.float32).astype(jnp.bfloat16)
    row_p = lax.broadcasted_iota(jnp.int32, (PAIR, 16), 0)
    lane_p = lax.broadcasted_iota(jnp.int32, (PAIR, 16), 1)
    pick_p = (row_p // ORB == lane_p).astype(jnp.bfloat16)
    pick_t = (row_p % ORB == lane_p).astype(jnp.bfloat16)
    below = lax.broadcasted_iota(jnp.int32, (half, half), 0) > lax.broadcasted_iota(jnp.int32, (half, half), 1)
    above = lax.broadcasted_iota(jnp.int32, (half, half), 0) < lax.broadcasted_iota(jnp.int32, (half, half), 1)

    sub = lax.broadcasted_iota(jnp.int32, (8, energies), 0)

    def atom(a, carry):
        held = [None, None]
        for k in range(NBR):
            index = a * NBR + k
            row = weight_ref[pl.ds(index, 1), :]
            turn = lax.rem(2 * energies - BAND // 2 - shift_ref[0, index], energies)
            tile = pltpu.roll(jnp.broadcast_to(row, (8, energies)), turn, 1)
            for step in (1, 2, 4):
                tile = jnp.where((sub & step) != 0, pltpu.roll(tile, step, 1), tile)
            band = jnp.concatenate([pltpu.roll(tile, 8 * b, 1) if b else tile for b in range(half // 8)], axis=0)
            near, far = band[:, :half], band[:, half:]
            near = near.astype(jnp.bfloat16)
            upper = jnp.where(below, far, 0.0).astype(jnp.bfloat16)
            lower = jnp.where(above, far, 0.0).astype(jnp.bfloat16)
            toeplitz = jnp.concatenate([
                jnp.concatenate([near, upper], axis=1),
                jnp.concatenate([lower, near], axis=1)], axis=0)
            partner = jnp.clip(near_ref[0, index] - first_atom, 0, 3 * per_dev - 1)
            block = green[pl.ds(pl.multiple_of(partner * BLOCK, 32), BLOCK), :]
            banded = jnp.dot(block, toeplitz, preferred_element_type=jnp.float32).astype(jnp.bfloat16)
            rows = pl.ds(pl.multiple_of(index * 16, 16), 16)
            left = jnp.dot(pick_p, spread_q[rows, :], preferred_element_type=jnp.float32)
            right = jnp.dot(pick_t, spread_r[rows, :], preferred_element_type=jnp.float32)
            both = (left * right).astype(jnp.bfloat16)
            for c in range(2):
                part = slice(c * PAIR, (c + 1) * PAIR)
                term = jnp.dot(both, banded[part], preferred_element_type=jnp.float32)
                if k % 2 == 0:
                    held[c] = term
                elif k == 1:
                    total[part, :] = held[c] + term
                else:
                    total[part, :] += held[c] + term
        return carry

    for a in range(per_dev):
        atom(a, 0)
        out_ref[:, a * BLOCK:(a + 1) * BLOCK] = total[...].T.astype(jnp.bfloat16)


def on_device(green_blocks, couplings, band_weights, neighbours, shifts):
    groups = lax.axis_size("energy")
    slabs = lax.axis_size("slab")
    local_e, slab_count = green_blocks.shape[3:]
    per_dev = slab_count // groups
    energies = local_e * groups
    width = per_dev * BLOCK
    pairs = per_dev * NBR
    assert per_dev == HALO
    vmem = pl.BlockSpec(memory_space=pltpu.VMEM)
    smem = pl.BlockSpec(memory_space=pltpu.SMEM)
    blocks = jax.ShapeDtypeStruct((groups, local_e, width), jnp.bfloat16)
    wide = pltpu.VMEM((pl.cdiv(slab_count, 128), BLOCK * local_e, 128), jnp.float32)
    packed = pltpu.VMEM((width // 128, energies, 128), jnp.float32)
    room = pltpu.CompilerParams(vmem_limit_bytes=32 * 1024 * 1024)
    sent = pl.pallas_call(
        functools.partial(pack_kernel, groups, per_dev),
        out_shape=blocks, in_specs=[vmem], out_specs=vmem,
        scratch_shapes=[wide, packed], compiler_params=room,
    )(green_blocks.reshape(BLOCK * local_e, slab_count))
    def exchanged(value, number):
        return pl.pallas_call(
            functools.partial(gather_kernel, groups),
            out_shape=blocks,
            in_specs=[vmem],
            out_specs=vmem,
            scratch_shapes=[
                pltpu.SemaphoreType.DMA((groups,)),
                pltpu.SemaphoreType.DMA((groups,)),
            ],
            compiler_params=pltpu.CompilerParams(
                collective_id=number, has_side_effects=True, vmem_limit_bytes=32 * 1024 * 1024),
        )(value)

    own = exchanged(sent, 0).reshape(energies, width)
    chain = [g * slabs + s for s in range(slabs) for g in range(groups)]
    up = list(zip(chain[:-1], chain[1:]))
    left = lax.ppermute(own, ("energy", "slab"), up)
    right = lax.ppermute(own, ("energy", "slab"), [(j, i) for i, j in up])

    weight = jnp.pad(band_weights.reshape(BAND, pairs)[::-1].T, ((0, 0), (0, energies - BAND)))
    matrix = couplings.reshape(ORB, ORB, pairs).transpose(2, 0, 1)
    matrix = jnp.pad(matrix, ((0, 0), (0, 16 - ORB), (0, 128 - ORB))).reshape(pairs * 16, 128)
    out = pl.pallas_call(
        scatter_kernel,
        out_shape=jax.ShapeDtypeStruct((energies, width), jnp.bfloat16),
        in_specs=[smem, smem, vmem, vmem, vmem, vmem, vmem],
        out_specs=vmem,
        scratch_shapes=[
            pltpu.VMEM((3 * width, energies), jnp.bfloat16),
            pltpu.VMEM((pairs * 16, PAIR), jnp.bfloat16),
            pltpu.VMEM((pairs * 16, PAIR), jnp.bfloat16),
            pltpu.VMEM((BLOCK, energies), jnp.float32),
        ],
        compiler_params=pltpu.CompilerParams(vmem_limit_bytes=40 * 1024 * 1024),
    )(neighbours, shifts, left, own, right, weight, matrix)
    landed = exchanged(out.reshape(groups, local_e, width), 1)
    back = pl.pallas_call(
        functools.partial(unpack_kernel, groups, per_dev),
        out_shape=jax.ShapeDtypeStruct((BLOCK * local_e, slab_count), jnp.bfloat16),
        in_specs=[vmem], out_specs=vmem,
        scratch_shapes=[packed, wide], compiler_params=room,
    )(landed)
    return back.reshape(2, ORB, ORB, local_e, slab_count)


def solution(mesh):
    return jax.shard_map(
        on_device,
        mesh=mesh,
        in_specs=(
            P(None, None, None, "energy", "slab"),
            P(None, None, "slab", "energy"),
            P(None, "slab", "energy"),
            P("slab", "energy"),
            P("slab", "energy"),
        ),
        out_specs=P(None, None, None, "energy", "slab"),
        check_vma=False,
    )
```
